32 devices in a mesh: grp: 4 (over x, core), dev: 8 (over z, y).
Axes of the slice: x: 2, y: 2, z: 4, core: 2. Of those that a mesh axis runs over, the one named last changes fastest.
Arguments:
- points: float32 [32768, 128], P(('grp', 'dev')), may hold values from -0.6 to 0.6
- weights: float32 [32768, 128], P(('grp', 'dev')), may hold values from -0.12 to 0.12
- skel_index: int32 [32, 128], P(('grp', 'dev')), may hold values from 0 to 1023
- projection: float32 [32, 128, 1024], P(('grp', 'dev')), may hold values from -0.1875 to 0.1875
- top_index: int32 [4, 256], P('grp'), may hold values from 0 to 1023
- subtree_projection: float32 [4, 256, 1024], P('grp', None, 'dev'), may hold values from -0.1875 to 0.1875
- near_leaf_mask: int32 [32, 3], P(('grp', 'dev')), may hold values from 0 to 1, as said below
Outputs:
- potential: float32 [32768, 128], P(('grp', 'dev'))
The draws below stay inside these ranges and needn't reach their ends.
Inputs may be any that keep to these rules, and one draw needn't show every extreme that they name: `near_leaf_mask`: entry [l, 1] (the leaf itself) is 1; entries that name a leaf outside the subtree are 0.
All inputs are finite; a program needn't handle non-finite values.
Results may differ from the reference program's by a relative error of at most 0.0003.
Values sent between devices are 32-bit elements; how exact they have to be, the bound alone decides.
A program may use at most 64 MiB of HBM per device.

```python
import jax
import jax.numpy as jnp
from jax import lax

D = 128
R = 128
LEAF = 1024
SKEL = 128
SKEL_TOP = 256
LEAF_DEV = 1
GROUPS = 4
LEAVES = 32
POINTS = 32768
CANDS = 1024
N_GRP = 4
N_DEV = 8


def draw_near_leaf_mask(key, part):
    first, second = jax.random.split(jax.random.fold_in(key, 7))
    devices = N_GRP * N_DEV
    slots = 3 * LEAF_DEV
    level = jax.random.randint(first, (devices,), 1, 9)
    noise = jax.random.randint(second, (devices, LEAF_DEV, slots), 0, 8)
    live = (noise < level[:, None, None]).astype(jnp.int32)
    slot_ids = jnp.arange(slots, dtype=jnp.int32)[None, None, :]
    target = jnp.arange(LEAF_DEV, dtype=jnp.int32)[None, :, None]
    position = (jnp.arange(devices, dtype=jnp.int32) % N_DEV)[:, None, None]
    outside = (position == 0) & (slot_ids < LEAF_DEV) | (position == N_DEV - 1) & (slot_ids >= 2 * LEAF_DEV)
    live = jnp.where(outside, 0, live)
    live = jnp.where(slot_ids == LEAF_DEV + target, 1, live)
    return live.reshape(devices * LEAF_DEV, slots)


def touch_ends(values, rng, low, largest):
    place = [jax.random.randint(jax.random.fold_in(rng, axis), (), 0, length) for axis, length in enumerate(values.shape)]
    main_axis = values.shape.index(max(values.shape))
    next_to = place[:main_axis] + [(place[main_axis] + 1) % values.shape[main_axis]] + place[main_axis + 1:]
    return values.at[tuple(place)].set(low).at[tuple(next_to)].set(largest)


def block_levels(own_key, extent, cuts, least, largest):
    gain = 1.0
    for dim, parts in cuts:
        steps = jax.random.uniform(jax.random.fold_in(jax.random.fold_in(own_key, 6), dim), (parts,), jnp.float32, least / len(cuts), largest / len(cuts))
        gain = gain * jnp.repeat(jnp.exp(steps), extent[dim] // parts).reshape((-1,) + (1,) * (len(extent) - 1 - dim))
    return gain


def normal_values(own_key, extent, deviation, reach, shards=(), kind=jnp.bfloat16):
    values = jax.random.normal(own_key, extent, jnp.float32) * deviation
    if len(shards) > 0:
        values = block_levels(own_key, extent, shards, -0.22, 0.18) * values
    return jnp.clip(values, min=-reach, max=reach).astype(kind)


def setup_inputs(seed: int = 0) -> dict:
    key_of = jax.random.split(jax.random.key(seed), 8)
    points = normal_values(key_of[0], (POINTS, D), 0.1, 0.6, ((0, 32),), jnp.float32)
    weights = normal_values(key_of[1], (POINTS, R), 0.02, 0.12, ((0, 32),), jnp.float32)
    skel_index = touch_ends(jax.random.randint(key_of[2], (LEAVES, SKEL), 0, LEAF), jax.random.fold_in(key_of[2], 1), 0, LEAF - 1).astype(jnp.int32)
    projection = normal_values(key_of[3], (LEAVES, SKEL, LEAF), LEAF ** -0.5, 0.1875, ((0, 32),), jnp.float32)
    top_index = touch_ends(jax.random.randint(key_of[4], (GROUPS, SKEL_TOP), 0, CANDS), jax.random.fold_in(key_of[4], 1), 0, CANDS - 1).astype(jnp.int32)
    subtree_projection = normal_values(key_of[5], (GROUPS, SKEL_TOP, CANDS), CANDS ** -0.5, 0.1875, ((0, 4), (2, 8)), jnp.float32)
    near_leaf_mask = draw_near_leaf_mask(jax.random.fold_in(key_of[7], 71), 0)
    return dict(points=points, weights=weights, skel_index=skel_index, projection=projection, top_index=top_index, subtree_projection=subtree_projection, near_leaf_mask=near_leaf_mask)


PRECISION_HIGH = lax.Precision.HIGHEST


def kernel_tile(left, right):
    left_sq = jnp.sum(left * left, axis=1)
    right_sq = jnp.sum(right * right, axis=1)
    cross = jnp.dot(left, right.T, precision=PRECISION_HIGH, preferred_element_type=jnp.float32)
    return jnp.exp(-0.5 * (left_sq[:, None] + right_sq[None, :] - 2.0 * cross))


def pick_rows(table, index):
    return table[index]


def reference(points, weights, skel_index, projection, top_index, subtree_projection, near_leaf_mask):
    leaves = points.shape[0] // LEAF
    per_group = LEAF_DEV * N_DEV
    groups = leaves // per_group
    slots = 3 * LEAF_DEV
    leaf_pts = points.reshape(leaves, LEAF, D)
    leaf_weight_values = weights.reshape(leaves, LEAF, R)
    skeleton_point_rows = jax.vmap(pick_rows)(leaf_pts, skel_index)
    skeleton_weight_values = jnp.einsum("vct,vta->vca", projection, leaf_weight_values, precision=PRECISION_HIGH)
    cand_pts = skeleton_point_rows.reshape(groups, per_group * SKEL, D)
    cand_wts = skeleton_weight_values.reshape(groups, per_group * SKEL, R)
    top_pts = jax.vmap(pick_rows)(cand_pts, top_index).reshape(groups * SKEL_TOP, D)
    top_wts = jnp.einsum("gtc,gcr->gtr", subtree_projection, cand_wts, precision=PRECISION_HIGH).reshape(groups * SKEL_TOP, R)
    top_group = jnp.arange(groups * SKEL_TOP, dtype=jnp.int32) // SKEL_TOP
    cand_leaf = jnp.arange(per_group * SKEL, dtype=jnp.int32) // SKEL
    slot_ids = jnp.arange(slots, dtype=jnp.int32)

    def one_leaf(leaf):
        group = leaf // per_group
        inner = leaf % per_group
        base = (inner // LEAF_DEV - 1) * LEAF_DEV
        target = leaf_pts[leaf]
        mask = near_leaf_mask[leaf].astype(jnp.float32)
        total = jnp.zeros((LEAF, R), jnp.float32)
        for slot in range(slots):
            source = group * per_group + jnp.clip(base + slot, 0, per_group - 1)
            term = jnp.dot(kernel_tile(target, leaf_pts[source]), leaf_weight_values[source], precision=PRECISION_HIGH, preferred_element_type=jnp.float32)
            total = total + mask[slot] * term
        hits = (cand_leaf[:, None] == base + slot_ids[None, :]).astype(jnp.float32)
        near_col = jnp.sum(hits * mask[None, :], axis=1)
        far_w = cand_wts[group] * (1.0 - near_col)[:, None]
        total = total + jnp.dot(kernel_tile(target, cand_pts[group]), far_w, precision=PRECISION_HIGH, preferred_element_type=jnp.float32)
        top_w = top_wts * (top_group != group).astype(jnp.float32)[:, None]
        total = total + jnp.dot(kernel_tile(target, top_pts), top_w, precision=PRECISION_HIGH, preferred_element_type=jnp.float32)
        return total

    result = lax.map(one_leaf, jnp.arange(leaves, dtype=jnp.int32))
    return result.reshape(leaves * LEAF, R)
```

```python
import functools
import math

import jax
import jax.numpy as jnp
from jax import lax
from jax.experimental import pallas as pl
from jax.experimental.pallas import tpu as pltpu
from jax.sharding import PartitionSpec as P

F32 = jnp.float32
BF16 = jnp.bfloat16
ROOT = math.sqrt(math.log2(math.e))
TILE = 256
BLOCK = 512
CHUNKS = 4


def split2(x):
    hi = x.astype(BF16)
    return hi, (x - hi.astype(F32)).astype(BF16)


def split3(x):
    hi = x.astype(BF16)
    rest = x - hi.astype(F32)
    mid = rest.astype(BF16)
    return hi, mid, (rest - mid.astype(F32)).astype(BF16)


def dot(a, b, dims=((1,), (0,))):
    return lax.dot_general(a, b, (dims, ((), ())), preferred_element_type=F32)


def dot3(a, b):
    n = b.shape[1]
    ah, al = split2(a)
    bh, bl = split2(b)
    both = dot(ah, jnp.concatenate([bh, bl], axis=1))
    return both[:, :n] + both[:, n:] + dot(al, bh)


def norm_columns(x, first):
    rows, feats = x.shape
    norm = -0.5 * jnp.sum(x * x, axis=1, keepdims=True)
    parts = [v.astype(F32) for v in split3(norm)]
    lane = lax.broadcasted_iota(jnp.int32, (rows, feats), 1)
    out = jnp.where((lane >= 3 - first) & (lane < 6 - first), 1.0, 0.0).astype(F32)
    for i, part in enumerate(parts):
        out = jnp.where(lane == first + i, part, out)
    return out.astype(BF16)


def kernel(
    n_grp, n_dev,
    pts, wts, skel_idx, proj, top_idx, sub, mask, out,
    left, right, right_w, acc, near, skel, slab, top_p, top_w,
    near_send, near_recv, skel_send, skel_recv, slab_send, slab_recv,
    row_send, row_recv, tp_send, tp_recv, tw_send, tw_recv,
):
    leaf, feats = pts.shape
    rhs = wts.shape[1]
    n_skel = skel_idx.shape[1]
    n_top = top_idx.shape[1]
    top_rows = n_top // n_dev
    g = lax.axis_index("grp")
    p = lax.axis_index("dev")
    half = n_dev // 2
    h = p // 2
    odd = p % 2
    partner = p + 1 - 2 * odd
    step_rows = leaf // CHUNKS

    def remote(src, dst, send, recv, dev=None, grp=None):
        return pltpu.make_async_remote_copy(
            src_ref=src, dst_ref=dst, send_sem=send, recv_sem=recv,
            device_id=(g if grp is None else grp, p if dev is None else dev),
            device_id_type=pl.DeviceIdType.MESH,
        )

    barrier = pltpu.get_barrier_semaphore()
    dev_peers = [lax.rem(p + k, n_dev) for k in range(1, n_dev)]
    grp_peers = [lax.rem(g + k, n_grp) for k in range(1, n_grp)]
    for q in dev_peers:
        pl.semaphore_signal(barrier, inc=1, device_id=(g, q), device_id_type=pl.DeviceIdType.MESH)
    for q in grp_peers:
        pl.semaphore_signal(barrier, inc=1, device_id=(q, p), device_id_type=pl.DeviceIdType.MESH)
    pl.semaphore_wait(barrier, len(dev_peers) + len(grp_peers))

    ahead = p + 2 - 4 * odd
    behind = p - 2 + 4 * odd
    can_send = (ahead >= 0) & (ahead < n_dev)
    can_recv = (behind >= 0) & (behind < n_dev)

    def near_first(c, part):
        rows = pl.ds(c * step_rows, step_rows)
        src = pts if part == 0 else wts
        return remote(
            src.at[rows], near.at[0, part, rows],
            near_send.at[0, part, c], near_recv.at[0, part, c], dev=partner,
        )

    def near_second(c, part):
        rows = pl.ds(c * step_rows, step_rows)
        return remote(
            near.at[0, part, rows], near.at[1, part, rows],
            near_send.at[1, part, c], near_recv.at[1, part, c], dev=ahead,
        )

    def start_first(c):
        near_first(c, 0).start()
        near_first(c, 1).start()

    def pass_on(c):
        for part in range(2):
            near_first(c, part).wait_recv()

            @pl.when(can_send)
            def _():
                near_second(c, part).start()

    def wait_second(c):
        @pl.when(can_recv)
        def _():
            for part in range(2):
                near_second(c, part).wait_recv()

    def skel_copy(owner, way, dev):
        return remote(
            skel.at[owner], skel.at[owner], skel_send.at[way, owner], skel_recv.at[owner], dev=dev
        )

    def skel_up(owner):
        @pl.when(h + 1 < half)
        def _():
            skel_copy(owner, 0, p + 2).start()

    def skel_down(owner):
        @pl.when(h > 0)
        def _():
            skel_copy(owner, 1, p - 2).start()

    def skel_step(s):
        @pl.when(h - s >= 0)
        def _():
            for side in range(2):
                owner = 2 * (h - s) + side
                skel_copy(owner, 0, partner).wait_recv()
                skel_up(owner)

        @pl.when(h + s < half)
        def _():
            for side in range(2):
                owner = 2 * (h + s) + side
                skel_copy(owner, 1, partner).wait_recv()
                skel_down(owner)

    def slab_copy(q, owner):
        return remote(
            sub.at[0, pl.ds(pl.multiple_of(q * top_rows, top_rows), top_rows)],
            slab.at[owner], slab_send.at[q], slab_recv.at[owner], dev=q,
        )

    for q in dev_peers:
        slab_copy(q, p).start()
    start_first(0)

    row = lax.broadcasted_iota(jnp.int32, (leaf, n_skel), 0)
    pick = jnp.where(row == skel_idx[...], 1.0, 0.0).astype(BF16)
    picked = dot(pick, jnp.concatenate(split3(pts[...]), axis=1), ((0,), (0,)))
    skel[p, 0] = picked[:, :feats] + picked[:, feats:2 * feats] + picked[:, 2 * feats:]
    skel[p, 1] = dot3(proj[0], wts[...])
    skel_copy(p, 2, partner).start()
    skel_up(p)
    skel_down(p)
    start_first(1)

    a = pts[...] * ROOT
    ah, al = split2(a)
    left[:, :feats] = ah
    left[:, feats:2 * feats] = al
    left[:, 2 * feats:3 * feats] = ah
    left[:, 3 * feats:] = norm_columns(a, 0)
    acc[...] = jnp.zeros_like(acc)

    def apply(first, source, weight):
        rows = pl.ds(first, source.shape[0])
        b = source * ROOT
        bh, bl = split2(b)
        right[rows, :feats] = bh
        right[rows, feats:2 * feats] = bh
        right[rows, 2 * feats:3 * feats] = bl
        right[rows, 3 * feats:] = norm_columns(b, 3)
        wh, wl = split2(weight)
        right_w[rows, :rhs] = wh
        right_w[rows, rhs:] = wl

    def run(width):
        def tile(i, carry):
            rows = pl.ds(pl.multiple_of(i * TILE, TILE), TILE)
            k = jnp.exp2(dot(left[rows], right[:width], ((1,), (1,))))
            kh, kl = split2(k)
            w = right_w[:width]
            acc[rows] += dot(kh, w) + dot(kl, w)
            return carry

        lax.fori_loop(0, leaf // TILE, tile, 0)

    def near_scale(k):
        return mask[0, k].astype(F32)

    blocks = []

    def self_block(i):
        rows = pl.ds(i * BLOCK, BLOCK)
        apply(0, pts[rows], wts[rows] * near_scale(1))
        run(BLOCK)

    per = BLOCK // step_rows

    def partner_block(i):
        rows = pl.ds(i * BLOCK, BLOCK)
        scale = jnp.where(odd == 1, near_scale(0), near_scale(2))
        apply(0, near[0, 0, rows], near[0, 1, rows] * scale)
        run(BLOCK)

    def other_block(i):
        for c in range(i * per, (i + 1) * per):
            wait_second(c)

        @pl.when(can_recv)
        def _():
            rows = pl.ds(i * BLOCK, BLOCK)
            scale = jnp.where(odd == 1, near_scale(2), near_scale(0))
            apply(0, near[1, 0, rows], near[1, 1, rows] * scale)
            run(BLOCK)

    leaves = BLOCK // n_skel

    def far_block(i):
        for j in range(leaves):
            owner = i * leaves + j
            keep = jnp.float32(1.0)
            for k in range(3):
                keep = keep - jnp.where(owner == p - 1 + k, near_scale(k), 0.0)
            apply(j * n_skel, skel[owner, 0], skel[owner, 1] * keep)
        run(BLOCK)

    self_block(0)
    skel_copy(partner, 2, partner).wait_recv()
    skel_up(partner)
    skel_down(partner)
    pass_on(0)
    start_first(2)
    self_block(1)
    for s in range(1, half):
        skel_step(s)
        if s == 1:
            pass_on(1)
            start_first(3)
            partner_block(0)

    def top_pick(j, total):
        ids = lax.broadcasted_iota(jnp.int32, (n_skel, n_top), 0) + j * n_skel
        one = jnp.where(ids == top_idx[...], 1.0, 0.0).astype(BF16)
        got = dot(one, jnp.concatenate(split3(skel[j, 0]), axis=1), ((0,), (0,)))
        return total + (got[:, :feats] + got[:, feats:2 * feats] + got[:, 2 * feats:])

    top_p[g] = lax.fori_loop(0, n_dev, top_pick, jnp.zeros((n_top, feats), F32))
    for q in grp_peers:
        remote(top_p.at[g], top_p.at[g], tp_send.at[q], tp_recv.at[g], grp=q).start()
    for q in dev_peers:
        slab_copy(p, q).wait_recv()
    slab[p] = sub[0, pl.ds(pl.multiple_of(p * top_rows, top_rows), top_rows)]

    def top_weight(j, total):
        return total + dot3(slab[j], skel[j, 1])

    top_w[g, p] = lax.fori_loop(0, n_dev, top_weight, jnp.zeros((top_rows, rhs), F32))
    for q in dev_peers:
        remote(top_w.at[g, p], top_w.at[g, p], row_send.at[q], row_recv.at[p], dev=q).start()

    far_block(0)
    for q in dev_peers:
        remote(top_w.at[g, q], top_w.at[g, q], row_send.at[q], row_recv.at[q], dev=q).wait_recv()
    for q in grp_peers:
        remote(top_w.at[g], top_w.at[g], tw_send.at[q], tw_recv.at[g], grp=q).start()
    pass_on(2)
    far_rest = n_dev // leaves
    if far_rest > 1:
        @pl.loop(1, far_rest)
        def _(i):
            far_block(i)
    pass_on(3)
    partner_block(1)
    other_block(0)
    for q in grp_peers:
        remote(top_p.at[q], top_p.at[q], tp_send.at[q], tp_recv.at[q], grp=q).wait_recv()
        remote(top_w.at[q], top_w.at[q], tw_send.at[q], tw_recv.at[q], grp=q).wait_recv()
        apply(0, top_p[q], top_w[q].reshape(n_top, rhs))
        run(n_top)
    other_block(1)
    out[...] = acc[:, :rhs] + acc[:, rhs:]

    for c in range(CHUNKS):
        for part in range(2):
            near_first(c, part).wait_send()

            @pl.when(can_send)
            def _():
                near_second(c, part).wait_send()
    skel_copy(p, 2, partner).wait_send()

    @pl.when(h + 1 < half)
    def _():
        @pl.loop(0, 2 * h + 2)
        def _(owner):
            skel_copy(owner, 0, p + 2).wait_send()

    @pl.when(h > 0)
    def _():
        @pl.loop(2 * h, n_dev)
        def _(owner):
            skel_copy(owner, 1, p - 2).wait_send()

    for q in dev_peers:
        slab_copy(q, p).wait_send()
        remote(top_w.at[g, p], top_w.at[g, p], row_send.at[q], row_recv.at[p], dev=q).wait_send()
    for q in grp_peers:
        remote(top_p.at[g], top_p.at[g], tp_send.at[q], tp_recv.at[g], grp=q).wait_send()
        remote(top_w.at[g], top_w.at[g], tw_send.at[q], tw_recv.at[g], grp=q).wait_send()


def solution(mesh):
    n_grp, n_dev = mesh.shape["grp"], mesh.shape["dev"]

    def local(points, weights, skel_index, projection, top_index, subtree_projection, near_leaf_mask):
        leaf, feats = points.shape
        rhs = weights.shape[1]
        n_skel = skel_index.shape[1]
        n_top = top_index.shape[1]
        vmem = pl.BlockSpec(memory_space=pltpu.VMEM)
        dma = pltpu.SemaphoreType.DMA
        return pl.pallas_call(
            functools.partial(kernel, n_grp, n_dev),
            out_shape=jax.ShapeDtypeStruct((leaf, rhs), F32),
            in_specs=[vmem] * 6 + [pl.BlockSpec(memory_space=pltpu.SMEM)],
            out_specs=vmem,
            scratch_shapes=[
                pltpu.VMEM((leaf, 4 * feats), BF16),
                pltpu.VMEM((BLOCK, 4 * feats), BF16),
                pltpu.VMEM((BLOCK, 2 * rhs), BF16),
                pltpu.VMEM((leaf, 2 * rhs), F32),
                pltpu.VMEM((2, 2, leaf, feats), F32),
                pltpu.VMEM((n_dev, 2, n_skel, feats), F32),
                pltpu.VMEM((n_dev, n_top // n_dev, n_skel), F32),
                pltpu.VMEM((n_grp, n_top, feats), F32),
                pltpu.VMEM((n_grp, n_dev, n_top // n_dev, rhs), F32),
                dma((2, 2, CHUNKS)), dma((2, 2, CHUNKS)),
                dma((3, n_dev)), dma((n_dev,)),
                dma((n_dev,)), dma((n_dev,)),
                dma((n_dev,)), dma((n_dev,)),
                dma((n_grp,)), dma((n_grp,)),
                dma((n_grp,)), dma((n_grp,)),
            ],
            compiler_params=pltpu.CompilerParams(
                collective_id=0, has_side_effects=True, vmem_limit_bytes=48 * 1024 * 1024
            ),
        )(points, weights, skel_index, projection, top_index, subtree_projection, near_leaf_mask)

    return jax.shard_map(
        local,
        mesh=mesh,
        in_specs=(
            P(("grp", "dev"), None),
            P(("grp", "dev"), None),
            P(("grp", "dev"), None),
            P(("grp", "dev"), None, None),
            P("grp", None),
            P("grp", None, "dev"),
            P(("grp", "dev"), None),
        ),
        out_specs=P(("grp", "dev"), None),
        check_vma=False,
    )
```

```python
import functools
import math

import jax
import jax.numpy as jnp
from jax import lax
from jax.experimental import pallas as pl
from jax.experimental.pallas import tpu as pltpu
from jax.sharding import PartitionSpec as P

F32 = jnp.float32
BF16 = jnp.bfloat16
ROOT = math.sqrt(math.log2(math.e))
TILE = 256
BLOCK = 512
CHUNKS = 4


def split2(x):
    hi = x.astype(BF16)
    return hi, (x - hi.astype(F32)).astype(BF16)


def split3(x):
    hi = x.astype(BF16)
    rest = x - hi.astype(F32)
    mid = rest.astype(BF16)
    return hi, mid, (rest - mid.astype(F32)).astype(BF16)


def dot(a, b, dims=((1,), (0,))):
    return lax.dot_general(a, b, (dims, ((), ())), preferred_element_type=F32)


def dot3(a, b):
    n = b.shape[1]
    ah, al = split2(a)
    bh, bl = split2(b)
    both = dot(ah, jnp.concatenate([bh, bl], axis=1))
    return both[:, :n] + both[:, n:] + dot(al, bh)


def norm_columns(x, first):
    rows, feats = x.shape
    norm = -0.5 * jnp.sum(x * x, axis=1, keepdims=True)
    parts = [v.astype(F32) for v in split3(norm)]
    lane = lax.broadcasted_iota(jnp.int32, (rows, feats), 1)
    out = jnp.where((lane >= 3 - first) & (lane < 6 - first), 1.0, 0.0).astype(F32)
    for i, part in enumerate(parts):
        out = jnp.where(lane == first + i, part, out)
    return out.astype(BF16)


def kernel(
    n_grp, n_dev,
    pts_in, wts_in, skel_idx_in, proj_in, top_idx_in, sub_in, mask_in, out,
    pts, wts, skel_idx, proj, top_idx, sub, mask,
    left, right, right_w, acc, near, skel, part_w, slab, top_p, top_w,
    load, near_send, near_recv, skel_send, skel_recv, slab_send, slab_recv,
    row_send, row_recv, tp_send, tp_recv, tw_send, tw_recv,
):
    leaf, feats = pts.shape
    rhs = wts.shape[1]
    n_skel = skel_idx.shape[1]
    n_top = top_idx.shape[1]
    top_rows = n_top // n_dev
    g = lax.axis_index("grp")
    p = lax.axis_index("dev")
    half = n_dev // 2
    h = p // 2
    odd = p % 2
    partner = p + 1 - 2 * odd
    step_rows = leaf // CHUNKS

    def remote(src, dst, send, recv, dev=None, grp=None):
        return pltpu.make_async_remote_copy(
            src_ref=src, dst_ref=dst, send_sem=send, recv_sem=recv,
            device_id=(g if grp is None else grp, p if dev is None else dev),
            device_id_type=pl.DeviceIdType.MESH,
        )

    loads = [
        pltpu.make_async_copy(src, dst, load.at[i])
        for i, (src, dst) in enumerate(
            [(skel_idx_in, skel_idx), (pts_in, pts), (proj_in, proj), (wts_in, wts),
             (sub_in, sub), (top_idx_in, top_idx), (mask_in, mask)]
        )
    ]
    for copy in loads:
        copy.start()
    barrier = pltpu.get_barrier_semaphore()
    dev_peers = [lax.rem(p + k, n_dev) for k in range(1, n_dev)]
    grp_peers = [lax.rem(g + k, n_grp) for k in range(1, n_grp)]
    for q in dev_peers:
        pl.semaphore_signal(barrier, inc=1, device_id=(g, q), device_id_type=pl.DeviceIdType.MESH)
    for q in grp_peers:
        pl.semaphore_signal(barrier, inc=1, device_id=(q, p), device_id_type=pl.DeviceIdType.MESH)
    pl.semaphore_wait(barrier, len(dev_peers) + len(grp_peers))

    ahead = p + 2 - 4 * odd
    behind = p - 2 + 4 * odd
    can_send = (ahead >= 0) & (ahead < n_dev)
    can_recv = (behind >= 0) & (behind < n_dev)

    def near_first(c, part):
        rows = pl.ds(c * step_rows, step_rows)
        src = pts_in if part == 0 else wts_in
        return remote(
            src.at[rows], near.at[0, part, rows],
            near_send.at[0, part, c], near_recv.at[0, part, c], dev=partner,
        )

    def near_second(c, part):
        rows = pl.ds(c * step_rows, step_rows)
        return remote(
            near.at[0, part, rows], near.at[1, part, rows],
            near_send.at[1, part, c], near_recv.at[1, part, c], dev=ahead,
        )

    def start_first(c):
        near_first(c, 0).start()
        near_first(c, 1).start()

    def pass_on(c):
        for part in range(2):
            near_first(c, part).wait_recv()

            @pl.when(can_send)
            def _():
                near_second(c, part).start()

    def wait_second(c):
        @pl.when(can_recv)
        def _():
            for part in range(2):
                near_second(c, part).wait_recv()

    def skel_copy(owner, way, dev):
        return remote(
            skel.at[owner], skel.at[owner], skel_send.at[way, owner], skel_recv.at[owner], dev=dev
        )

    def skel_up(owner):
        @pl.when(h + 1 < half)
        def _():
            skel_copy(owner, 0, p + 2).start()

    def skel_down(owner):
        @pl.when(h > 0)
        def _():
            skel_copy(owner, 1, p - 2).start()

    def skel_step(s):
        @pl.when(h - s >= 0)
        def _():
            for side in range(2):
                owner = 2 * (h - s) + side
                skel_copy(owner, 0, partner).wait_recv()
                skel_up(owner)

        @pl.when(h + s < half)
        def _():
            for side in range(2):
                owner = 2 * (h + s) + side
                skel_copy(owner, 1, partner).wait_recv()
                skel_down(owner)

    def slab_copy(q, owner):
        return remote(part_w.at[q], slab.at[owner], slab_send.at[q], slab_recv.at[owner], dev=q)

    def row_copy(q, owner):
        return remote(
            top_w.at[g, owner], top_w.at[g, owner], row_send.at[q], row_recv.at[owner], dev=q
        )

    relay = n_grp == 4
    mate = g + 1 - 2 * (g % 2)
    across = lax.rem(g + 2, 4)
    far_mate = lax.rem(mate + 2, 4)

    def grp_copy(top, sems, q, owner, slot):
        return remote(top.at[owner], top.at[owner], sems[0].at[slot], sems[1].at[owner], grp=q)

    tp_sems, tw_sems = (tp_send, tp_recv), (tw_send, tw_recv)

    def grp_start(top, sems):
        if relay:
            grp_copy(top, sems, across, g, 1).start()
            grp_copy(top, sems, mate, g, 0).start()
        else:
            for q in grp_peers:
                grp_copy(top, sems, q, g, q).start()

    def grp_relay(top, sems):
        if relay:
            grp_copy(top, sems, across, across, 1).wait_recv()
            grp_copy(top, sems, mate, across, 2).start()

    def grp_wait(top, sems, k):
        if relay:
            if k > 0:
                owner = (mate, far_mate)[k - 1]
                grp_copy(top, sems, mate, owner, 0).wait_recv()
        else:
            grp_copy(top, sems, grp_peers[k], grp_peers[k], grp_peers[k]).wait_recv()

    grp_order = [across, mate, far_mate] if relay else grp_peers

    def grp_sent(top, sems):
        if relay:
            grp_copy(top, sems, across, g, 1).wait_send()
            grp_copy(top, sems, mate, g, 0).wait_send()
            grp_copy(top, sems, mate, across, 2).wait_send()
        else:
            for q in grp_peers:
                grp_copy(top, sems, q, g, q).wait_send()

    start_first(0)
    for copy in loads:
        copy.wait()

    row = lax.broadcasted_iota(jnp.int32, (leaf, n_skel), 0)
    pick = jnp.where(row == skel_idx[...], 1.0, 0.0).astype(BF16)
    picked = dot(pick, jnp.concatenate(split3(pts[...]), axis=1), ((0,), (0,)))
    skel[p, 0] = picked[:, :feats] + picked[:, feats:2 * feats] + picked[:, 2 * feats:]
    skel[p, 1] = dot3(proj[0], wts[...])
    skel_copy(p, 2, partner).start()
    skel_up(p)
    skel_down(p)
    part_w[...] = dot3(sub[0], skel[p, 1]).reshape(n_dev, top_rows, rhs)
    for q in dev_peers:
        slab_copy(q, p).start()
    start_first(1)

    a = pts[...] * ROOT
    ah, al = split2(a)
    left[:, :feats] = ah
    left[:, feats:2 * feats] = al
    left[:, 2 * feats:3 * feats] = ah
    left[:, 3 * feats:] = norm_columns(a, 0)
    acc[...] = jnp.zeros_like(acc)

    def apply(first, source, weight):
        rows = pl.ds(first, source.shape[0])
        b = source * ROOT
        bh, bl = split2(b)
        right[rows, :feats] = bh
        right[rows, feats:2 * feats] = bh
        right[rows, 2 * feats:3 * feats] = bl
        right[rows, 3 * feats:] = norm_columns(b, 3)
        wh, wl = split2(weight)
        right_w[rows, :rhs] = wh
        right_w[rows, rhs:] = wl

    def run(width):
        def tile(i, carry):
            rows = pl.ds(pl.multiple_of(i * TILE, TILE), TILE)
            k = jnp.exp2(dot(left[rows], right[:width], ((1,), (1,))))
            kh, kl = split2(k)
            w = right_w[:width]
            acc[rows] += dot(kh, w) + dot(kl, w)
            return carry

        lax.fori_loop(0, leaf // TILE, tile, 0, unroll=True)

    def near_scale(k):
        return mask[0, k].astype(F32)

    blocks = []

    def self_block(i):
        rows = pl.ds(i * BLOCK, BLOCK)
        apply(0, pts[rows], wts[rows] * near_scale(1))
        run(BLOCK)

    per = BLOCK // step_rows

    def partner_block(i):
        rows = pl.ds(i * BLOCK, BLOCK)
        scale = jnp.where(odd == 1, near_scale(0), near_scale(2))
        apply(0, near[0, 0, rows], near[0, 1, rows] * scale)
        run(BLOCK)

    def other_block(i):
        for c in range(i * per, (i + 1) * per):
            wait_second(c)

        @pl.when(can_recv)
        def _():
            rows = pl.ds(i * BLOCK, BLOCK)
            scale = jnp.where(odd == 1, near_scale(2), near_scale(0))
            apply(0, near[1, 0, rows], near[1, 1, rows] * scale)
            run(BLOCK)

    leaves = BLOCK // n_skel

    def far_block(i):
        for j in range(leaves):
            owner = i * leaves + j
            keep = jnp.float32(1.0)
            for k in range(3):
                keep = keep - jnp.where(owner == p - 1 + k, near_scale(k), 0.0)
            apply(j * n_skel, skel[owner, 0], skel[owner, 1] * keep)
        run(BLOCK)

    self_block(0)
    skel_copy(partner, 2, partner).wait_recv()
    skel_up(partner)
    skel_down(partner)
    pass_on(0)
    start_first(2)
    total = part_w[p]
    for q in dev_peers:
        slab_copy(p, q).wait_recv()
        total = total + slab[q]
    top_w[g, p] = total
    for q in dev_peers:
        row_copy(q, p).start()
    self_block(1)
    skel_step(1)
    pass_on(1)
    start_first(3)
    for q in dev_peers:
        row_copy(q, q).wait_recv()
    grp_start(top_w, tw_sems)
    for s in range(2, half):
        skel_step(s)
        if s == 2:
            partner_block(0)

    def top_pick(j, total):
        ids = lax.broadcasted_iota(jnp.int32, (n_skel, n_top), 0) + j * n_skel
        one = jnp.where(ids == top_idx[...], 1.0, 0.0).astype(BF16)
        got = dot(one, jnp.concatenate(split3(skel[j, 0]), axis=1), ((0,), (0,)))
        return total + (got[:, :feats] + got[:, feats:2 * feats] + got[:, 2 * feats:])

    top_p[g] = lax.fori_loop(0, n_dev, top_pick, jnp.zeros((n_top, feats), F32))
    grp_start(top_p, tp_sems)
    grp_relay(top_w, tw_sems)
    pass_on(2)

    @pl.loop(0, n_dev // leaves)
    def _(i):
        far_block(i)

    grp_relay(top_p, tp_sems)
    other_block(0)
    pass_on(3)
    partner_block(1)
    for k, q in enumerate(grp_order):
        grp_wait(top_p, tp_sems, k)
        grp_wait(top_w, tw_sems, k)
        apply(0, top_p[q], top_w[q].reshape(n_top, rhs))
        run(n_top)
    other_block(1)
    out[...] = acc[:, :rhs] + acc[:, rhs:]

    for c in range(CHUNKS):
        for part in range(2):
            near_first(c, part).wait_send()

            @pl.when(can_send)
            def _():
                near_second(c, part).wait_send()
    skel_copy(p, 2, partner).wait_send()

    @pl.when(h + 1 < half)
    def _():
        @pl.loop(0, 2 * h + 2)
        def _(owner):
            skel_copy(owner, 0, p + 2).wait_send()

    @pl.when(h > 0)
    def _():
        @pl.loop(2 * h, n_dev)
        def _(owner):
            skel_copy(owner, 1, p - 2).wait_send()

    for q in dev_peers:
        slab_copy(q, p).wait_send()
        row_copy(q, p).wait_send()
    grp_sent(top_p, tp_sems)
    grp_sent(top_w, tw_sems)


def solution(mesh):
    n_grp, n_dev = mesh.shape["grp"], mesh.shape["dev"]

    def local(points, weights, skel_index, projection, top_index, subtree_projection, near_leaf_mask):
        leaf, feats = points.shape
        rhs = weights.shape[1]
        n_skel = skel_index.shape[1]
        n_top = top_index.shape[1]
        vmem = pl.BlockSpec(memory_space=pltpu.VMEM)
        hbm = pl.BlockSpec(memory_space=pltpu.HBM)
        dma = pltpu.SemaphoreType.DMA
        return pl.pallas_call(
            functools.partial(kernel, n_grp, n_dev),
            out_shape=jax.ShapeDtypeStruct((leaf, rhs), F32),
            in_specs=[hbm] * 7,
            out_specs=vmem,
            scratch_shapes=[
                pltpu.VMEM(points.shape, F32),
                pltpu.VMEM(weights.shape, F32),
                pltpu.VMEM(skel_index.shape, jnp.int32),
                pltpu.VMEM(projection.shape, F32),
                pltpu.VMEM(top_index.shape, jnp.int32),
                pltpu.VMEM(subtree_projection.shape, F32),
                pltpu.SMEM(near_leaf_mask.shape, jnp.int32),
                pltpu.VMEM((leaf, 4 * feats), BF16),
                pltpu.VMEM((BLOCK, 4 * feats), BF16),
                pltpu.VMEM((BLOCK, 2 * rhs), BF16),
                pltpu.VMEM((leaf, 2 * rhs), F32),
                pltpu.VMEM((2, 2, leaf, feats), F32),
                pltpu.VMEM((n_dev, 2, n_skel, feats), F32),
                pltpu.VMEM((n_dev, n_top // n_dev, rhs), F32),
                pltpu.VMEM((n_dev, n_top // n_dev, rhs), F32),
                pltpu.VMEM((n_grp, n_top, feats), F32),
                pltpu.VMEM((n_grp, n_dev, n_top // n_dev, rhs), F32),
                dma((7,)),
                dma((2, 2, CHUNKS)), dma((2, 2, CHUNKS)),
                dma((3, n_dev)), dma((n_dev,)),
                dma((n_dev,)), dma((n_dev,)),
                dma((n_dev,)), dma((n_dev,)),
                dma((n_grp,)), dma((n_grp,)),
                dma((n_grp,)), dma((n_grp,)),
            ],
            compiler_params=pltpu.CompilerParams(
                collective_id=0, has_side_effects=True, vmem_limit_bytes=48 * 1024 * 1024
            ),
        )(points, weights, skel_index, projection, top_index, subtree_projection, near_leaf_mask)

    return jax.shard_map(
        local,
        mesh=mesh,
        in_specs=(
            P(("grp", "dev"), None),
            P(("grp", "dev"), None),
            P(("grp", "dev"), None),
            P(("grp", "dev"), None, None),
            P("grp", None),
            P("grp", None, "dev"),
            P(("grp", "dev"), None),
        ),
        out_specs=P(("grp", "dev"), None),
        check_vma=False,
    )
```
